128 devices in a mesh: dp: 8 (over z_lo, x), mp: 16 (over z_hi, y, core).
Axes of the slice: x: 4, y: 4, z: 4 (z_hi: 2, z_lo: 2; z = z_hi * 2 + z_lo), core: 2. Of those that a mesh axis runs over, the one named last changes fastest.
Arguments:
- tokens: bfloat16 [3072, 1024], P('dp', 'mp'), may hold values from -6 to 6
- grad_out: bfloat16 [3072, 1024], P('dp', 'mp'), may hold values from -6 to 6
- hidden_pre: bfloat16 [3072, 65536], P('dp', 'mp'), may hold values from -6 to 6
- w_in: bfloat16 [1024, 65536], P(None, 'mp'), may hold values from -0.1875 to 0.1875
- w_out: bfloat16 [65536, 1024], P('mp'), may hold values from -0.0234375 to 0.0234375
- row_in: float32 [1024], P('dp'), may hold values from 1 to 100
- col_in: float32 [65536], P('mp'), may hold values from 1 to 100
- row_out: float32 [65536], P('mp'), may hold values from 30 to 3000
- col_out: float32 [1024], P('dp'), may hold values from 30 to 3000
Outputs:
- grad_tokens: bfloat16 [3072, 1024], P('dp', 'mp')
- step_in: float32 [1024, 65536], P('dp', 'mp')
- step_out: float32 [65536, 1024], P('mp', 'dp')
- new_row_in: float32 [1024], P('dp')
- new_col_in: float32 [65536], P('mp')
- new_row_out: float32 [65536], P('mp')
- new_col_out: float32 [1024], P('dp')
The draws below stay inside these ranges and needn't reach their ends.
All inputs are finite; a program needn't handle non-finite values.
Results may differ from the reference program's by a relative error of at most 0.0049.
Values may be sent and summed in bfloat16 or wider, within the bound.
A program may use at most 192 MiB of HBM per device.

```python
import math
import jax
import jax.numpy as jnp
from jax import lax

D = 1024
FF = 65536
TOKENS = 3072


def block_scale(rng, shape, split, smallest, top_value):
    loudness = 1.0
    for axis_at, shards_of in split:
        heights = jax.random.uniform(jax.random.fold_in(jax.random.fold_in(rng, 6), axis_at), (shards_of,), jnp.float32, smallest / len(split), top_value / len(split))
        loudness = loudness * jnp.repeat(jnp.exp(heights), shape[axis_at] // shards_of).reshape((-1,) + (1,) * (len(shape) - 1 - axis_at))
    return loudness


def gaussian(own_key, extent, deviation, reach, cuts=(), kind=jnp.bfloat16):
    drawn = deviation * jax.random.normal(own_key, extent, jnp.float32)
    if cuts:
        drawn = drawn * block_scale(own_key, extent, cuts, -0.22, 0.18)
    return jnp.clip(drawn, -reach, reach).astype(kind)


def setup_inputs(seed: int = 0) -> dict:
    keys = jax.random.split(jax.random.key(seed), 10)
    tokens = gaussian(keys[0], (TOKENS, D), 1.0, 6.0, ((0, 8), (1, 16)))
    grad_out = gaussian(keys[1], (TOKENS, D), 1.0, 6.0, ((0, 8), (1, 16)))
    hidden_pre = gaussian(keys[2], (TOKENS, FF), 1.0, 6.0, ((0, 8), (1, 16)))
    w_in = gaussian(keys[3], (D, FF), D ** -0.5, 0.1875, ((1, 16),))
    w_out = gaussian(keys[4], (FF, D), FF ** -0.5, 0.0234375, ((0, 16),))
    row_in = jnp.clip(jnp.exp(math.log(100.0) - 4.6051702 * jax.random.uniform(keys[5], (D,), jnp.float32) ** block_scale(keys[5], (D,), ((0, 8),), -0.2, 0.2)), 1.0, 100.0)
    col_in = jnp.clip(jnp.exp(math.log(100.0) - 4.6051702 * jax.random.uniform(keys[6], (FF,), jnp.float32) ** block_scale(keys[6], (FF,), ((0, 16),), -0.2, 0.2)), 1.0, 100.0)
    row_out = jnp.clip(jnp.exp(math.log(3000.0) - 4.6051702 * jax.random.uniform(keys[7], (FF,), jnp.float32) ** block_scale(keys[7], (FF,), ((0, 16),), -0.2, 0.2)), 30.0, 3000.0)
    col_out = jnp.clip(jnp.exp(math.log(3000.0) - 4.6051702 * jax.random.uniform(keys[8], (D,), jnp.float32) ** block_scale(keys[8], (D,), ((0, 8),), -0.2, 0.2)), 30.0, 3000.0)
    return {"tokens": tokens, "grad_out": grad_out, "hidden_pre": hidden_pre, "w_in": w_in, "w_out": w_out, "row_in": row_in, "col_in": col_in, "row_out": row_out, "col_out": col_out}


def precondition(grads, row_acc, col_acc):
    nu = jnp.minimum(row_acc[:, None], col_acc[None, :]) + grads * grads
    return (grads / jnp.sqrt(nu), lax.optimization_barrier(jnp.max(nu, axis=1)), lax.optimization_barrier(jnp.max(nu, axis=0)))

def reference(tokens, grad_out, hidden_pre, w_in, w_out, row_in, col_in, row_out, col_out):
    relu_out = jnp.maximum(hidden_pre, jnp.zeros_like(hidden_pre))
    back = jnp.dot(grad_out, w_out.T, preferred_element_type=jnp.float32)
    hidden_grad = jnp.where(hidden_pre > 0, back, jnp.float32(0.0)).astype(jnp.bfloat16)
    grad_tokens = jnp.dot(hidden_grad, w_in.T, preferred_element_type=jnp.float32).astype(jnp.bfloat16)
    grad_in = jnp.dot(tokens.T, hidden_grad, preferred_element_type=jnp.float32)
    grad_wout = jnp.dot(relu_out.T, grad_out, preferred_element_type=jnp.float32)
    step_in, new_row_in, new_col_in = precondition(grad_in, row_in, col_in)
    step_out, new_row_out, new_col_out = precondition(grad_wout, row_out, col_out)
    return (grad_tokens, step_in, step_out, new_row_in, new_col_in, new_row_out, new_col_out)
```

```python
import jax
import jax.numpy as jnp
from jax import lax
from jax.experimental import pallas as pl
from jax.experimental.pallas import tpu as pltpu
from jax.sharding import PartitionSpec as P

MESH = pl.DeviceIdType.MESH
F32, BF16 = jnp.float32, jnp.bfloat16

TOK = 384
FF = 4096
D = 1024
W = 256
K = FF // W
DELTA = 2
LAG_D = 1
LAG_F = 3
RING = 4
AHEAD = 3
HALF = K // 2


def nt(left, right):
    return lax.dot_general(left, right, (((1,), (1,)), ((), ())), preferred_element_type=F32)


def kernel(
    blk, hid_hbm, win_hbm, wout_hbm, row_in, col_in, row_out, col_out,
    gt_out, step_in, step_out, new_row_in, new_col_in, new_row_out, new_col_out,
    hid, win, wout, gath, dy, lhs, hgo, hgb, gtacc,
    f_send, f_recv, n_send, n_recv, d_send, d_recv, keep_d, keep_0,
    gs1, gr1, gs2, gk2, gr2, gs3, gk3, gr3,
    rb, rowm, colm, colr, colm2, colr2, rm1, rr1, rm2, rr2, rm3, rr3,
    load_sem, z_ss, z_rs, s_ss, s_rs, y_ss, y_rs, c_ss, c_rs,
    f_ss, f_rs, n_ss, n_rs, d_ss, d_rs, g_ss, g_rs, e_ss, e_rs,
):
    dp = lax.axis_index("dp")
    mp = lax.axis_index("mp")
    zlo, x = dp // 4, dp % 4
    zhi, y, c = mp // 8, (mp // 2) % 4, mp % 2

    def dev(zlo_, x_, zhi_, y_, c_):
        return (zlo_ * 4 + x_, zhi_ * 8 + y_ * 2 + c_)

    x_peer = [dev(zlo, (x + i) % 4, zhi, y, c) for i in range(4)]
    y_peer = [dev(zlo, x, zhi, (y + i) % 4, c) for i in range(4)]
    zlo_peer = dev(1 - zlo, x, zhi, y, c)
    zhi_peer = dev(zlo, x, 1 - zhi, y, c)
    diag_peer = dev(1 - zlo, x, 1 - zhi, y, c)
    core_peer = dev(zlo, x, zhi, y, 1 - c)

    def remote(src, dst, ss, rs, peer):
        return pltpu.make_async_remote_copy(
            src_ref=src, dst_ref=dst, send_sem=ss, recv_sem=rs, device_id=peer, device_id_type=MESH
        )

    loads = [
        pltpu.make_async_copy(hid_hbm, hid.at[pl.ds(zlo * TOK, TOK)], load_sem.at[0]),
        pltpu.make_async_copy(wout_hbm, wout, load_sem.at[1]),
        pltpu.make_async_copy(win_hbm, win, load_sem.at[2]),
    ]
    for load in loads:
        load.start()

    barrier = pltpu.get_barrier_semaphore()
    peers = x_peer[1:] + y_peer[1:] + [zlo_peer, zhi_peer, diag_peer, core_peer]
    for peer in peers:
        pl.semaphore_signal(barrier, inc=1, device_id=peer, device_id_type=MESH)
    pl.semaphore_wait(barrier, len(peers))

    piece = gath.at[zhi, y, c, zlo]
    s1 = remote(blk, piece, s_ss.at[0], s_rs.at[0], zlo_peer)
    s2 = remote(blk, piece, s_ss.at[1], s_rs.at[1], diag_peer)
    s1.start()
    s2.start()

    def z_copy(k):
        cols = pl.ds(pl.multiple_of(k * W, W), W)
        return remote(
            hid_hbm.at[:, cols], hid.at[pl.ds(zlo * TOK, TOK), cols], z_ss.at[k], z_rs.at[k], zlo_peer
        )

    for k in range(AHEAD):
        z_copy(k).start()
    piece[...] = blk[...]
    s1.wait_recv()
    other = gath.at[zhi, y, c, 1 - zlo]
    s3 = remote(other, other, s_ss.at[2], s_rs.at[2], diag_peer)
    s3.start()
    s2.wait_recv()
    s3.wait_recv()

    def rows_of(stage):
        return (zlo, pl.ds(64, 64)) if stage == 0 else (zlo, pl.ds(0, 64)) if stage == 1 else (1 - zlo, pl.ds(64, 64))

    def y_copy(stage, i):
        h, rows = rows_of(stage)
        part = gath.at[h, y, c, :, rows]
        return remote(part, part, y_ss.at[stage, i - 1], y_rs.at[stage, i - 1], y_peer[i])

    def c_copy(stage):
        h, rows = rows_of(stage)
        part = gath.at[h, :, c, :, rows]
        return remote(part, part, c_ss.at[stage], c_rs.at[stage], core_peer)

    for stage in range(3):
        for i in (1, 3, 2):
            y_copy(stage, i).start()

    def row_block(row):
        return jnp.broadcast_to(row[...], (128, 128)).T

    rb[0] = row_block(row_in)
    rb[1] = row_block(col_out)
    rowm[...] = jnp.zeros_like(rowm)

    def finish_gather(stage):
        for i in (1, 2, 3):
            y_copy(stage, i).wait_recv()
        c_copy(stage).start()
        c_copy(stage).wait_recv()

    def assemble(mat):
        for r in range(4):
            owner = (x + r) % 4
            for core in range(2):
                for lo in range(2):
                    lhs[mat, pl.ds(r * 128 + core * 64, 64), pl.ds(lo * TOK, TOK)] = gath[
                        zlo, owner, core, lo, pl.ds(64 * mat, 64), :
                    ]

    def transpose_dy():
        for h in range(2):
            for yy in range(4):
                for lo in range(2):
                    both = jnp.concatenate(
                        [gath[h, yy, 0, lo, 64:128, :], gath[h, yy, 1, lo, 64:128, :]], axis=0
                    )
                    dy[pl.ds(lo * TOK, TOK), pl.ds((h * 4 + yy) * 128, 128)] = both.astype(F32).T.astype(BF16)

    finish_gather(0)
    assemble(1)
    loads[0].wait()
    loads[1].wait()

    toward = [(x_peer[1], x_peer[3]), (x_peer[3], x_peer[1])]

    def f_copy(mat, k):
        return remote(f_send.at[mat, k], f_recv.at[mat, k], f_ss.at[mat, k], f_rs.at[mat, k], toward[mat][0])

    def n_copy(mat, k):
        return remote(n_send.at[mat, k], n_recv.at[mat, k], n_ss.at[mat, k], n_rs.at[mat, k], toward[mat][1])

    def d_copy(mat, k):
        return remote(d_send.at[mat, k], d_recv.at[mat, k], d_ss.at[mat, k], d_rs.at[mat, k], toward[mat][0])

    def products(mat, k, right):
        part = jnp.dot(lhs[mat], right, preferred_element_type=F32)
        near, back = (3, 1) if mat == 0 else (1, 3)
        slot = k % RING
        f_send[mat, k] = part[256:384].astype(BF16)
        f_copy(mat, k).start()
        n_send[mat, k] = part[near * 128 : near * 128 + 128].astype(BF16)
        n_copy(mat, k).start()
        keep_d[mat, slot] = part[back * 128 : back * 128 + 128]
        keep_0[mat, slot] = part[0:128]

    def pass_on(mat, k):
        f_copy(mat, k).wait_recv()
        d_send[mat, k] = (keep_d[mat, k % RING] + f_recv[mat, k].astype(F32)).astype(BF16)
        d_copy(mat, k).start()

    def finish(mat, k):
        n_copy(mat, k).wait_recv()
        d_copy(mat, k).wait_recv()
        lanes = col_in if mat == 0 else row_out
        for h in range(W // 128):
            cut = pl.ds(h * 128, 128)
            g = (
                keep_0[mat, k % RING, :, cut]
                + n_recv[mat, k, :, cut].astype(F32)
                + d_recv[mat, k, :, cut].astype(F32)
            )
            block = k * (W // 128) + h
            nu = jnp.minimum(rb[mat], lanes[pl.ds(block, 1), :]) + g * g
            step = g * lax.rsqrt(nu)
            at = pl.ds(pl.multiple_of(block * 128, 128), 128)
            if mat == 0:
                step_in[:, at] = step
            else:
                step_out[at, :] = step.T
            rowm[mat] = jnp.maximum(rowm[mat], nu)
            colm[pl.ds(mat * (FF // 128) + block, 1), :] = jnp.max(nu, axis=0, keepdims=True)
        f_copy(mat, k).wait_send()
        n_copy(mat, k).wait_send()
        d_copy(mat, k).wait_send()

    def hidden_grad(lo, k):
        cols = pl.ds(pl.multiple_of(k * W, W), W)
        rows = pl.ds(pl.multiple_of(lo * TOK, TOK), TOK)
        back = nt(dy[rows, :], wout[cols, :])
        return jnp.where(hid[rows, cols] > 0, back, F32(0.0)).astype(BF16)

    def own_tokens(k):
        cols = pl.ds(pl.multiple_of(k * W, W), W)
        grad = hidden_grad(zlo, k)
        hgo[:, cols] = grad
        gtacc[...] += nt(win[:, cols], grad)

    def g_copy(i):
        if i == 0:
            return remote(gs1, gr1, g_ss.at[0], g_rs.at[0], core_peer)
        if i < 4:
            return remote(gs2.at[(y + i) % 4], gr2.at[i - 1], g_ss.at[i], g_rs.at[i], y_peer[i])
        return remote(gs3, gr3, g_ss.at[4], g_rs.at[4], zhi_peer)

    def gt_rows(j, core):
        return gtacc[pl.ds(pl.multiple_of(j * 128 + core * 64, 64), 64), :]

    def gt_stage(i):
        if i == 0:
            for j in range(8):
                gs1[j] = gt_rows(j, 1 - c).astype(BF16)
            g_copy(0).start()
        elif i == 1:
            g_copy(0).wait_recv()
            for h in range(2):
                for yy in range(4):
                    gs2[yy, h] = (gt_rows(h * 4 + yy, c) + gr1[h * 4 + yy].astype(F32)).astype(BF16)
                gk2[h] = gt_rows(h * 4 + y, c) + gr1[h * 4 + y].astype(F32)
            for j in (1, 2, 3):
                g_copy(j).start()
        elif i == 2:
            for j in (1, 2, 3):
                g_copy(j).wait_recv()

            def total(h):
                return gk2[h] + gr2[0, h].astype(F32) + gr2[1, h].astype(F32) + gr2[2, h].astype(F32)

            gs3[...] = total(1 - zhi).astype(BF16)
            gk3[...] = total(zhi)
            g_copy(4).start()
        else:
            g_copy(4).wait_recv()
            gt_out[...] = (gk3[...] + gr3[...].astype(F32)).astype(BF16)
            for j in range(5):
                g_copy(j).wait_send()

    def between(value, low, high):
        return jnp.logical_and(value >= low, value < high)

    def turn(i, carry):
        for mat, first in ((1, 0), (0, DELTA)):

            @pl.when(between(i - first - LAG_D, 0, K))
            def _():
                pass_on(mat, i - first - LAG_D)

            @pl.when(between(i - first - LAG_F, 0, K))
            def _():
                finish(mat, i - first - LAG_F)

        @pl.when(i < K)
        def _():
            z_copy(i).wait_recv()

            @pl.when(i + AHEAD < K)
            def _():
                z_copy(i + AHEAD).start()

            cols = pl.ds(pl.multiple_of(i * W, W), W)
            pre = hid[:, cols]
            products(1, i, jnp.maximum(pre, jnp.zeros_like(pre)))

        p = i - DELTA

        @pl.when(p == 0)
        def _():
            finish_gather(1)
            assemble(0)
            finish_gather(2)
            transpose_dy()
            loads[2].wait()
            gtacc[...] = jnp.zeros_like(gtacc)

        @pl.when(between(p, 0, HALF))
        def _():
            own_tokens(2 * p)
            own_tokens(2 * p + 1)

        @pl.when(between(p, 0, K))
        def _():
            cols = pl.ds(pl.multiple_of(p * W, W), W)
            hgb[pl.ds(pl.multiple_of(zlo * TOK, TOK), TOK), :] = hgo[:, cols]
            hgb[pl.ds(pl.multiple_of((1 - zlo) * TOK, TOK), TOK), :] = hidden_grad(1 - zlo, p)
            products(0, p, hgb[...])

        for s, at in enumerate((HALF, HALF + 1, HALF + 3, HALF + 5)):

            @pl.when(p == at)
            def _():
                gt_stage(s)

        return carry

    lax.fori_loop(0, K + DELTA + LAG_F, turn, 0)

    def e_copy(i):
        if i < 3:
            return remote(colm, colr.at[i], e_ss.at[i], e_rs.at[i], x_peer[i + 1])
        if i == 3:
            return remote(rm1, rr1, e_ss.at[3], e_rs.at[3], core_peer)
        if i == 4:
            return remote(colm2, colr2, e_ss.at[4], e_rs.at[4], zlo_peer)
        if i < 8:
            return remote(rm2, rr2.at[i - 5], e_ss.at[i], e_rs.at[i], y_peer[i - 4])
        return remote(rm3, rr3, e_ss.at[8], e_rs.at[8], zhi_peer)

    for i in range(3):
        e_copy(i).start()
    rm1[...] = jnp.zeros_like(rm1)
    for mat in range(2):
        rm1[mat : mat + 1, :] = jnp.max(rowm[mat].T, axis=0, keepdims=True)
    e_copy(3).start()
    e_copy(3).wait_recv()
    rm2[...] = jnp.maximum(rm1[...], rr1[...])
    for i in (5, 6, 7):
        e_copy(i).start()
    for i in range(3):
        e_copy(i).wait_recv()
    colm2[...] = jnp.maximum(jnp.maximum(colm[...], colr[0]), jnp.maximum(colr[1], colr[2]))
    e_copy(4).start()
    for i in (5, 6, 7):
        e_copy(i).wait_recv()
    rm3[...] = jnp.maximum(jnp.maximum(rm2[...], rr2[0]), jnp.maximum(rr2[1], rr2[2]))
    e_copy(8).start()
    e_copy(4).wait_recv()
    rows = FF // 128
    new_col_in[...] = jnp.maximum(colm2[0:rows], colr2[0:rows])
    new_row_out[...] = jnp.maximum(colm2[rows:], colr2[rows:])
    e_copy(8).wait_recv()
    new_row_in[...] = jnp.maximum(rm3[0:1], rr3[0:1])
    new_col_out[...] = jnp.maximum(rm3[1:2], rr3[1:2])

    for i in range(9):
        e_copy(i).wait_send()
    for copy in (s1, s2, s3):
        copy.wait_send()
    for stage in range(3):
        for i in (1, 2, 3):
            y_copy(stage, i).wait_send()
        c_copy(stage).wait_send()

    def z_sent(k, carry):
        z_copy(k).wait_send()
        return carry

    lax.fori_loop(0, K, z_sent, 0)


def on_device(tokens, grad_out, hidden_pre, w_in, w_out, row_in, col_in, row_out, col_out):
    blk = jnp.concatenate([tokens, grad_out], axis=1).T
    vmem = pl.BlockSpec(memory_space=pltpu.VMEM)
    hbm = pl.BlockSpec(memory_space=pl.ANY)
    dma = pltpu.SemaphoreType.DMA
    rows = FF // 128
    wire = pltpu.VMEM((2, K, 128, W), BF16)
    kept = pltpu.VMEM((2, RING, 128, W), F32)
    gt, step_in, step_out, nri, nci, nro, nco = pl.pallas_call(
        kernel,
        out_shape=(
            jax.ShapeDtypeStruct((64, TOK), BF16),
            jax.ShapeDtypeStruct((128, FF), F32),
            jax.ShapeDtypeStruct((FF, 128), F32),
            jax.ShapeDtypeStruct((1, 128), F32),
            jax.ShapeDtypeStruct((rows, 128), F32),
            jax.ShapeDtypeStruct((rows, 128), F32),
            jax.ShapeDtypeStruct((1, 128), F32),
        ),
        in_specs=[vmem, hbm, hbm, hbm, vmem, vmem, vmem, vmem],
        out_specs=(vmem,) * 7,
        scratch_shapes=[
            pltpu.VMEM((2 * TOK, FF), BF16),
            pltpu.VMEM((D, FF), BF16),
            pltpu.VMEM((FF, D), BF16),
            pltpu.VMEM((2, 4, 2, 2, 128, TOK), BF16),
            pltpu.VMEM((2 * TOK, D), BF16),
            pltpu.VMEM((2, 512, 2 * TOK), BF16),
            pltpu.VMEM((TOK, FF), BF16),
            pltpu.VMEM((2 * TOK, W), BF16),
            pltpu.VMEM((D, TOK), F32),
            wire, wire, wire, wire, wire, wire,
            kept, kept,
            pltpu.VMEM((8, 64, TOK), BF16),
            pltpu.VMEM((8, 64, TOK), BF16),
            pltpu.VMEM((4, 2, 64, TOK), BF16),
            pltpu.VMEM((2, 64, TOK), F32),
            pltpu.VMEM((3, 2, 64, TOK), BF16),
            pltpu.VMEM((64, TOK), BF16),
            pltpu.VMEM((64, TOK), F32),
            pltpu.VMEM((64, TOK), BF16),
            pltpu.VMEM((2, 128, 128), F32),
            pltpu.VMEM((2, 128, 128), F32),
            pltpu.VMEM((2 * rows, 128), F32),
            pltpu.VMEM((3, 2 * rows, 128), F32),
            pltpu.VMEM((2 * rows, 128), F32),
            pltpu.VMEM((2 * rows, 128), F32),
            pltpu.VMEM((8, 128), F32),
            pltpu.VMEM((8, 128), F32),
            pltpu.VMEM((8, 128), F32),
            pltpu.VMEM((3, 8, 128), F32),
            pltpu.VMEM((8, 128), F32),
            pltpu.VMEM((8, 128), F32),
            dma((3,)),
            dma((K,)), dma((K,)),
            dma((3,)), dma((3,)),
            dma((3, 3)), dma((3, 3)),
            dma((3,)), dma((3,)),
            dma((2, K)), dma((2, K)),
            dma((2, K)), dma((2, K)),
            dma((2, K)), dma((2, K)),
            dma((5,)), dma((5,)),
            dma((9,)), dma((9,)),
        ],
        compiler_params=pltpu.CompilerParams(
            collective_id=0, has_side_effects=True, vmem_limit_bytes=63 * 2**20
        ),
        name="ffn_backward",
    )(
        blk, hidden_pre, w_in, w_out,
        row_in.reshape(1, 128), col_in.reshape(rows, 128), row_out.reshape(rows, 128), col_out.reshape(1, 128),
    )
    return (
        gt.T, step_in, step_out,
        nri.reshape(128), nci.reshape(FF), nro.reshape(FF), nco.reshape(128),
    )


def solution(mesh):
    in_specs = (
        P("dp", "mp"),
        P("dp", "mp"),
        P("dp", "mp"),
        P(None, "mp"),
        P("mp", None),
        P("dp"),
        P("mp"),
        P("mp"),
        P("dp"),
    )
    out_specs = (P("dp", "mp"), P("dp", "mp"), P("mp", "dp"), P("dp"), P("mp"), P("mp"), P("dp"))
    return jax.shard_map(
        on_device, mesh=mesh, in_specs=in_specs, out_specs=out_specs, check_vma=False
    )
```

```python
import jax
import jax.numpy as jnp
from jax import lax
from jax.experimental import pallas as pl
from jax.experimental.pallas import tpu as pltpu
from jax.sharding import PartitionSpec as P

MESH = pl.DeviceIdType.MESH
F32, BF16 = jnp.float32, jnp.bfloat16

TOK = 384
FF = 4096
D = 1024
W = 256
K = FF // W
DELTA = 1
LAG_D = 2
LAG_F = 6
RING = 8
WSLOT = 4
SOON = 3 * FF // 512
AHEAD = 6
OWN_W = 512
OWN = FF // OWN_W


def nt(left, right):
    return lax.dot_general(left, right, (((1,), (1,)), ((), ())), preferred_element_type=F32)


def kernel(
    tok_t, dy_t, hid_hbm, win_hbm, wout_hbm, row_in, col_in, row_out, col_out,
    gt_out, steps_out, new_row_in, new_col_in, new_row_out, new_col_out,
    steps, hid, win, wout_slot, wout_t, gath, dy, lhs, hgo, hgb, gtacc,
    f_send, f_recv, n_send, d_send, nd_recv, keep_d, keep_0,
    gs1, gr1, gs2, gk2, gr2, gs3, gk3, gr3,
    rb, rowm, colm, colr, rm1, rr1, rm2, rr2,
    load_sem, wout_sem, step_sem, z_ss, z_rs, s_ss, s_rs, y_ss, y_rs, c_ss, c_rs,
    x_ss, f_rs, nd_rs, g_ss, g_rs, e_ss, e_rs, l_ss, l_rs, r_ss, r_rs,
):
    dp = lax.axis_index("dp")
    mp = lax.axis_index("mp")
    zlo, x = dp // 4, dp % 4
    zhi, y, c = mp // 8, (mp // 2) % 4, mp % 2

    def dev(zlo_, x_, zhi_, y_, c_):
        return (zlo_ * 4 + x_, zhi_ * 8 + y_ * 2 + c_)

    x_peer = [dev(zlo, (x + i) % 4, zhi, y, c) for i in range(4)]
    y_peer = [dev(zlo, x, zhi, (y + i) % 4, c) for i in range(4)]
    zlo_peer = dev(1 - zlo, x, zhi, y, c)
    zhi_peer = dev(zlo, x, 1 - zhi, y, c)
    diag_peer = dev(1 - zlo, x, 1 - zhi, y, c)
    core_peer = dev(zlo, x, zhi, y, 1 - c)
    dp_peer = [((dp + i) % 8, mp) for i in range(8)]
    pair_peer = dev(zlo, x, 1 - zhi, y, 1 - c)

    def remote(src, dst, ss, rs, peer):
        return pltpu.make_async_remote_copy(
            src_ref=src, dst_ref=dst, send_sem=ss, recv_sem=rs, device_id=peer, device_id_type=MESH
        )

    loads = [
        pltpu.make_async_copy(hid_hbm, hid.at[pl.ds(zlo * TOK, TOK)], load_sem.at[0]),
        pltpu.make_async_copy(win_hbm, win, load_sem.at[1]),
    ]

    def wout_load(k):
        rows = pl.ds(pl.multiple_of(k * W, W), W)
        return pltpu.make_async_copy(wout_hbm.at[rows], wout_slot.at[k % WSLOT], wout_sem.at[k % WSLOT])

    for k in range(WSLOT):
        wout_load(k).start()
    for load in loads:
        load.start()

    barrier = pltpu.get_barrier_semaphore()
    peers = dp_peer[1:] + y_peer[1:] + [core_peer, zhi_peer, pair_peer, diag_peer]
    for peer in peers:
        pl.semaphore_signal(barrier, inc=1, device_id=peer, device_id_type=MESH)
    pl.semaphore_wait(barrier, len(peers))

    toks, dys = pl.ds(0, 64), pl.ds(64, 64)

    def s_copy(i):
        own, rows = (dy_t, dys) if i < 3 else (tok_t, toks)
        peer = (zlo_peer, diag_peer, zhi_peer)[i % 3]
        return remote(own, gath.at[zhi, y, c, zlo, rows], s_ss.at[i], s_rs.at[i], peer)

    far = (zhi + zlo) % 2

    def place(piece):
        if isinstance(piece, int) and piece >= 4:
            return zlo, piece - 4, toks
        second = piece // 2
        lo = (zlo + piece + second) % 2
        return (zhi + second) % 2, lo, dys

    def y_copy(piece, i):
        h, lo, rows = place(piece)
        part = gath.at[h, y, c, lo, rows]
        return remote(part, part, y_ss.at[piece], y_rs.at[piece], y_peer[i])

    def y_all(piece):
        h, lo, rows = place(piece)
        part = gath.at[h, pl.ds(0, 3), c, lo, rows]
        return remote(part, part, y_ss.at[piece], y_rs.at[piece], y_peer[1])

    def c_copy(piece):
        h, lo, rows = place(piece)
        part = gath.at[h, :, c, lo, rows]
        return remote(part, part, c_ss.at[piece], c_rs.at[piece], core_peer)

    def y_start(piece):
        for i in (1, 3, 2):
            y_copy(piece, i).start()

    def z_copy(k):
        cols = pl.ds(pl.multiple_of(k * W, W), W)
        return remote(
            hid_hbm.at[:, cols], hid.at[pl.ds(zlo * TOK, TOK), cols], z_ss.at[0], z_rs.at[k], zlo_peer
        )

    for i in (0, 1, 2):
        s_copy(i).start()
    gath[zhi, y, c, zlo, dys] = dy_t[...]
    y_start(0)

    @pl.when(far == 0)
    def _():
        s_copy(5).start()

    @pl.when(far == 1)
    def _():
        s_copy(3).start()
        s_copy(4).start()

    for k in range(AHEAD):
        z_copy(k).start()

    gath[zhi, y, c, zlo, toks] = tok_t[...]

    @pl.when(far == 0)
    def _():
        s_copy(0).wait_recv()
        y_start(1)
        s_copy(1).wait_recv()
        y_start(2)
        s_copy(2).wait_recv()
        y_start(3)

    @pl.when(far == 1)
    def _():
        s_copy(1).wait_recv()
        y_start(2)
        s_copy(2).wait_recv()
        y_start(3)
        s_copy(0).wait_recv()
        y_start(1)

    @pl.when(far == 0)
    def _():
        s_copy(3).wait_recv()

    @pl.when(far == 1)
    def _():
        s_copy(4).wait_recv()
        s_copy(5).wait_recv()

    y_start(4)
    y_start(5)

    def row_block(row):
        return jnp.broadcast_to(row[...], (128, 128)).T

    rb[0] = row_block(row_in)
    rb[1] = row_block(col_out)
    rowm[...] = jnp.zeros_like(rowm)

    def pass_to_core(piece):
        y_all(piece).wait_recv()
        c_copy(piece).start()

    def assemble(mat):
        for r in range(4):
            owner = (x + r) % 4
            for core in range(2):
                for lo in range(2):
                    lhs[mat, pl.ds(r * 128 + core * 64, 64), pl.ds(lo * TOK, TOK)] = gath[
                        zlo, owner, core, lo, pl.ds(64 * mat, 64), :
                    ]

    def transpose_dy():
        for h in range(2):
            for yy in range(4):
                for lo in range(2):
                    both = jnp.concatenate(
                        [gath[h, yy, 0, lo, 64:128, :], gath[h, yy, 1, lo, 64:128, :]], axis=0
                    )
                    dy[pl.ds(lo * TOK, TOK), pl.ds((h * 4 + yy) * 128, 128)] = both.astype(F32).T.astype(BF16)

    def transpose_wout(k, carry):
        wout_load(k).wait()
        cols = pl.ds(pl.multiple_of(k * W, W), W)
        wout_t[:, cols] = wout_slot[k % WSLOT].T

        @pl.when(k + WSLOT < K)
        def _():
            wout_load(k + WSLOT).start()

        return carry

    lax.fori_loop(0, K // 2, transpose_wout, 0)
    first, rest = 2 * far, 2 * (1 - far)
    pass_to_core(first)
    pass_to_core(first + 1)
    c_copy(first).wait_recv()
    c_copy(first + 1).wait_recv()
    assemble(1)
    loads[0].wait()

    toward = [(x_peer[1], x_peer[3]), (x_peer[3], x_peer[1])]

    def f_copy(mat, k):
        return remote(f_send.at[mat, k], f_recv.at[mat, k], x_ss.at[0], f_rs.at[mat, k], toward[mat][0])

    def n_copy(mat, k):
        return remote(n_send.at[mat, k], nd_recv.at[mat, k, 0], x_ss.at[1], nd_rs.at[mat, k], toward[mat][1])

    def d_copy(mat, k):
        return remote(d_send.at[mat, k], nd_recv.at[mat, k, 1], x_ss.at[2], nd_rs.at[mat, k], toward[mat][0])

    def products(mat, k, right):
        part = jnp.dot(lhs[mat], right, preferred_element_type=F32)
        near, back = (3, 1) if mat == 0 else (1, 3)
        slot = k % RING
        f_send[mat, k] = part[256:384].astype(BF16)
        f_copy(mat, k).start()
        n_send[mat, k] = part[near * 128 : near * 128 + 128].astype(BF16)
        n_copy(mat, k).start()
        keep_d[mat, slot] = part[back * 128 : back * 128 + 128]
        keep_0[mat, slot] = part[0:128]

    def pass_on(mat, k):
        f_copy(mat, k).wait_recv()
        d_send[mat, k] = (keep_d[mat, k % RING] + f_recv[mat, k].astype(F32)).astype(BF16)
        d_copy(mat, k).start()

    def step_copy(mat, k):
        cols = pl.ds(pl.multiple_of(k * W, W), W)
        return pltpu.make_async_copy(steps.at[mat, :, cols], steps_out.at[mat, :, cols], step_sem.at[0])

    def finish(mat, k):
        both = nd_recv.at[mat, k]
        remote(both, both, x_ss.at[1], nd_rs.at[mat, k], toward[mat][1]).wait_recv()
        lanes = col_in if mat == 0 else row_out
        for h in range(W // 128):
            cut = pl.ds(h * 128, 128)
            g = (
                keep_0[mat, k % RING, :, cut]
                + nd_recv[mat, k, 0, :, cut].astype(F32)
                + nd_recv[mat, k, 1, :, cut].astype(F32)
            )
            block = k * (W // 128) + h
            nu = jnp.minimum(rb[mat], lanes[pl.ds(block, 1), :]) + g * g
            step = g * lax.rsqrt(nu)
            steps[mat, :, pl.ds(pl.multiple_of(block * 128, 128), 128)] = step.astype(BF16)
            rowm[mat] = jnp.maximum(rowm[mat], nu)
            last = block // SOON
            row = (1 - mat) * (SOON - last * (2 * SOON - FF // 128)) + last * SOON + block
            colm[pl.ds(row, 1), :] = jnp.max(nu, axis=0, keepdims=True)
        step_copy(mat, k).start()

    def hidden_grad(lo, start, width):
        cols = pl.ds(pl.multiple_of(start, width), width)
        rows = pl.ds(pl.multiple_of(lo * TOK, TOK), TOK)
        back = jnp.dot(dy[rows, :], wout_t[:, cols], preferred_element_type=F32)
        return jnp.where(hid[rows, cols] > 0, back, F32(0.0)).astype(BF16)

    def own_tokens(j):
        cols = pl.ds(pl.multiple_of(j * OWN_W, OWN_W), OWN_W)
        grad = hidden_grad(zlo, j * OWN_W, OWN_W)
        hgo[:, cols] = grad
        gtacc[...] += nt(win[:, cols], grad)

    def g_copy(i):
        if i == 0:
            return remote(gs1, gr1, g_ss.at[0], g_rs.at[0], core_peer)
        if i < 4:
            return remote(gs2.at[(y + i) % 4], gr2.at[i - 1], g_ss.at[1], g_rs.at[1], y_peer[i])
        return remote(gs3, gr3, g_ss.at[2], g_rs.at[2], zhi_peer)

    def g_all():
        return remote(gs2.at[pl.ds(0, 3)], gr2, g_ss.at[1], g_rs.at[1], y_peer[1])

    def gt_rows(j, core):
        return gtacc[pl.ds(pl.multiple_of(j * 128 + core * 64, 64), 64), :]

    def gt_stage(i):
        if i == 0:
            for j in range(8):
                gs1[j] = gt_rows(j, 1 - c).astype(BF16)
            g_copy(0).start()
        elif i == 1:
            g_copy(0).wait_recv()
            for h in range(2):
                for yy in range(4):
                    gs2[yy, h] = (gt_rows(h * 4 + yy, c) + gr1[h * 4 + yy].astype(F32)).astype(BF16)
                gk2[h] = gt_rows(h * 4 + y, c) + gr1[h * 4 + y].astype(F32)
            for j in (1, 2, 3):
                g_copy(j).start()
        elif i == 2:
            g_all().wait_recv()

            def total(h):
                return gk2[h] + gr2[0, h].astype(F32) + gr2[1, h].astype(F32) + gr2[2, h].astype(F32)

            gs3[...] = total(1 - zhi).astype(BF16)
            gk3[...] = total(zhi)
            g_copy(4).start()
        else:
            g_copy(4).wait_recv()
            gt_out[...] = (gk3[...] + gr3[...].astype(F32)).astype(BF16)
            g_copy(0).wait_send()
            g_all().wait_send()
            g_copy(4).wait_send()

    def between(value, low, high):
        return jnp.logical_and(value >= low, value < high)

    early, late = pl.ds(0, 2 * SOON), pl.ds(2 * SOON, 2 * FF // 128 - 2 * SOON)

    def early_copy(i):
        return remote(colm.at[early], colr.at[i - 1, early], e_ss.at[0], e_rs.at[0], dp_peer[i])

    def late_copy(i):
        return remote(colm.at[late], colr.at[i - 1, late], l_ss.at[0], l_rs.at[0], dp_peer[i])

    def turn(i, carry):
        for mat, first in ((1, 0), (0, DELTA)):

            @pl.when(between(i - first - LAG_D, 0, K))
            def _():
                pass_on(mat, i - first - LAG_D)

            @pl.when(between(i - first - LAG_F, 0, K))
            def _():
                finish(mat, i - first - LAG_F)

        @pl.when(i < K)
        def _():
            z_copy(i).wait_recv()

            @pl.when(i + AHEAD < K)
            def _():
                z_copy(i + AHEAD).start()

            cols = pl.ds(pl.multiple_of(i * W, W), W)
            pre = hid[:, cols]
            products(1, i, jnp.maximum(pre, jnp.zeros_like(pre)))

        p = i - DELTA

        @pl.when(p == 0)
        def _():
            for piece in (rest, rest + 1, 4, 5):
                pass_to_core(piece)
            c_copy(rest).wait_recv()
            c_copy(rest + 1).wait_recv()
            lax.fori_loop(K // 2, K, transpose_wout, 0)
            transpose_dy()
            c_copy(4).wait_recv()
            c_copy(5).wait_recv()
            assemble(0)
            loads[1].wait()
            gtacc[...] = jnp.zeros_like(gtacc)

        @pl.when(between(p, 0, OWN))
        def _():
            own_tokens(p)

        @pl.when(between(p, 0, K))
        def _():
            cols = pl.ds(pl.multiple_of(p * W, W), W)
            hgb[pl.ds(pl.multiple_of(zlo * TOK, TOK), TOK), :] = hgo[:, cols]
            hgb[pl.ds(pl.multiple_of((1 - zlo) * TOK, TOK), TOK), :] = hidden_grad(1 - zlo, p * W, W)
            products(0, p, hgb[...])

        for s, at in enumerate((OWN, OWN + 1, OWN + 3, OWN + 5)):

            @pl.when(p == at)
            def _():
                gt_stage(s)

        @pl.when(i == K * 3 // 4 - 1 + DELTA + LAG_F)
        def _():
            for j in range(1, 8):
                early_copy(j).start()

        return carry

    lax.fori_loop(0, K + DELTA + LAG_F, turn, 0)

    for i in range(1, 8):
        late_copy(i).start()
    rm1[...] = jnp.zeros_like(rm1)
    for mat in range(2):
        rm1[mat : mat + 1, :] = jnp.max(rowm[mat].T, axis=0, keepdims=True)

    def row_copy(i):
        if i < 3:
            return remote(rm1, rr1.at[i], r_ss.at[0], r_rs.at[0], (core_peer, zhi_peer, pair_peer)[i])
        return remote(rm2, rr2.at[i - 3], r_ss.at[1], r_rs.at[1], y_peer[i - 2])

    for i in range(3):
        row_copy(i).start()
    row_1 = remote(rr1, rr1, r_ss.at[0], r_rs.at[0], core_peer)
    row_2 = remote(rr2, rr2, r_ss.at[1], r_rs.at[1], y_peer[1])
    row_1.wait_recv()
    rm2[...] = jnp.maximum(jnp.maximum(rm1[...], rr1[0]), jnp.maximum(rr1[1], rr1[2]))
    for i in range(3, 6):
        row_copy(i).start()

    for i in range(3):
        s_copy(i).wait_send()

    @pl.when(far == 0)
    def _():
        s_copy(5).wait_send()

    @pl.when(far == 1)
    def _():
        s_copy(3).wait_send()
        s_copy(4).wait_send()

    for piece in range(6):
        y_all(piece).wait_send()
        c_copy(piece).wait_send()

    own_rows = hid.at[pl.ds(zlo * TOK, TOK)]
    remote(hid_hbm, own_rows, z_ss.at[0], z_rs.at[0], zlo_peer).wait_send()
    remote(f_send, f_recv, x_ss.at[0], f_rs.at[0, 0], x_peer[1]).wait_send()
    remote(n_send, f_recv, x_ss.at[1], f_rs.at[0, 0], x_peer[1]).wait_send()
    remote(d_send, f_recv, x_ss.at[2], f_rs.at[0, 0], x_peer[1]).wait_send()

    pltpu.make_async_copy(steps, steps_out, step_sem.at[0]).wait()

    remote(colr.at[:, early], colr.at[:, early], e_ss.at[0], e_rs.at[0], zlo_peer).wait()
    remote(colr.at[:, late], colr.at[:, late], l_ss.at[0], l_rs.at[0], zlo_peer).wait()
    top = colm[...]
    for i in range(7):
        top = jnp.maximum(top, colr[i])
    rest_rows = FF // 128 - SOON
    new_row_out[...] = jnp.concatenate([top[0:SOON], top[2 * SOON : 2 * SOON + rest_rows]], axis=0)
    new_col_in[...] = jnp.concatenate([top[SOON : 2 * SOON], top[2 * SOON + rest_rows :]], axis=0)
    row_1.wait_send()
    row_2.wait()
    top = jnp.maximum(jnp.maximum(rm2[...], rr2[0]), jnp.maximum(rr2[1], rr2[2]))
    new_row_in[...] = top[0:1]
    new_col_out[...] = top[1:2]


def write_out(steps_in, steps_out, gt, nri, nci, nro, nco, o_gt, o_in, o_out, o_nri, o_nci, o_nro, o_nco):
    o_in[...] = steps_in[0].astype(F32)
    o_out[...] = steps_out[0].astype(F32).T

    @pl.when(pl.program_id(0) == 0)
    def _():
        o_gt[...] = gt[...]
        o_nri[...] = nri[...]
        o_nci[...] = nci[...]
        o_nro[...] = nro[...]
        o_nco[...] = nco[...]


def on_device(tokens, grad_out, hidden_pre, w_in, w_out, row_in, col_in, row_out, col_out):
    vmem = pl.BlockSpec(memory_space=pltpu.VMEM)
    hbm = pl.BlockSpec(memory_space=pl.ANY)
    dma = pltpu.SemaphoreType.DMA
    rows = FF // 128
    wire = pltpu.VMEM((2, K, 128, W), BF16)
    kept = pltpu.VMEM((2, RING, 128, W), F32)
    small = (
        jax.ShapeDtypeStruct((64, TOK), BF16),
        jax.ShapeDtypeStruct((1, 128), F32),
        jax.ShapeDtypeStruct((rows, 128), F32),
        jax.ShapeDtypeStruct((rows, 128), F32),
        jax.ShapeDtypeStruct((1, 128), F32),
    )
    gt, steps, nri, nci, nro, nco = pl.pallas_call(
        kernel,
        out_shape=small[:1] + (jax.ShapeDtypeStruct((2, 128, FF), BF16),) + small[1:],
        in_specs=[vmem, vmem, hbm, hbm, hbm, vmem, vmem, vmem, vmem],
        out_specs=(vmem, hbm, vmem, vmem, vmem, vmem),
        scratch_shapes=[
            pltpu.VMEM((2, 128, FF), BF16),
            pltpu.VMEM((2 * TOK, FF), BF16),
            pltpu.VMEM((D, FF), BF16),
            pltpu.VMEM((WSLOT, W, D), BF16),
            pltpu.VMEM((D, FF), BF16),
            pltpu.VMEM((2, 4, 2, 2, 128, TOK), BF16),
            pltpu.VMEM((2 * TOK, D), BF16),
            pltpu.VMEM((2, 512, 2 * TOK), BF16),
            pltpu.VMEM((TOK, FF), BF16),
            pltpu.VMEM((2 * TOK, W), BF16),
            pltpu.VMEM((D, TOK), F32),
            wire, wire, wire, wire,
            pltpu.VMEM((2, K, 2, 128, W), BF16),
            kept, kept,
            pltpu.VMEM((8, 64, TOK), BF16),
            pltpu.VMEM((8, 64, TOK), BF16),
            pltpu.VMEM((4, 2, 64, TOK), BF16),
            pltpu.VMEM((2, 64, TOK), F32),
            pltpu.VMEM((3, 2, 64, TOK), BF16),
            pltpu.VMEM((64, TOK), BF16),
            pltpu.VMEM((64, TOK), F32),
            pltpu.VMEM((64, TOK), BF16),
            pltpu.VMEM((2, 128, 128), F32),
            pltpu.VMEM((2, 128, 128), F32),
            pltpu.VMEM((2 * rows, 128), F32),
            pltpu.VMEM((7, 2 * rows, 128), F32),
            pltpu.VMEM((8, 128), F32),
            pltpu.VMEM((3, 8, 128), F32),
            pltpu.VMEM((8, 128), F32),
            pltpu.VMEM((3, 8, 128), F32),
            dma((2,)), dma((WSLOT,)), dma((1,)),
            dma((1,)), dma((K,)),
            dma((6,)), dma((6,)),
            dma((6,)), dma((6,)),
            dma((6,)), dma((6,)),
            dma((3,)), dma((2, K)), dma((2, K)),
            dma((3,)), dma((3,)),
            dma((1,)), dma((1,)),
            dma((1,)), dma((1,)),
            dma((2,)), dma((2,)),
        ],
        compiler_params=pltpu.CompilerParams(
            collective_id=0, has_side_effects=True, vmem_limit_bytes=63 * 2**20
        ),
        name="ffn_backward",
    )(
        tokens.T, grad_out.T, hidden_pre, w_in, w_out,
        row_in.reshape(1, 128), col_in.reshape(rows, 128), row_out.reshape(rows, 128), col_out.reshape(1, 128),
    )

    parts = 2
    wide = FF // parts

    def whole(shape):
        return pl.BlockSpec(shape.shape, lambda j: (0,) * len(shape.shape))

    gt, step_in, step_out, nri, nci, nro, nco = pl.pallas_call(
        write_out,
        grid=(parts,),
        out_shape=small[:1]
        + (jax.ShapeDtypeStruct((128, FF), F32), jax.ShapeDtypeStruct((FF, 128), F32))
        + small[1:],
        in_specs=[
            pl.BlockSpec((1, 128, wide), lambda j: (0, 0, j)),
            pl.BlockSpec((1, 128, wide), lambda j: (1, 0, j)),
        ]
        + [whole(shape) for shape in small],
        out_specs=(
            whole(small[0]),
            pl.BlockSpec((128, wide), lambda j: (0, j)),
            pl.BlockSpec((wide, 128), lambda j: (j, 0)),
        )
        + tuple(whole(shape) for shape in small[1:]),
        name="write_out",
    )(steps, steps, gt, nri, nci, nro, nco)
    return (
        gt.T, step_in, step_out,
        nri.reshape(128), nci.reshape(FF), nro.reshape(FF), nco.reshape(128),
    )


def solution(mesh):
    in_specs = (
        P("dp", "mp"),
        P("dp", "mp"),
        P("dp", "mp"),
        P(None, "mp"),
        P("mp", None),
        P("dp"),
        P("mp"),
        P("mp"),
        P("dp"),
    )
    out_specs = (P("dp", "mp"), P("dp", "mp"), P("mp", "dp"), P("dp"), P("mp"), P("mp"), P("dp"))
    return jax.shard_map(
        on_device, mesh=mesh, in_specs=in_specs, out_specs=out_specs, check_vma=False
    )
```

```python
import jax
import jax.numpy as jnp
from jax import lax
from jax.experimental import pallas as pl
from jax.experimental.pallas import tpu as pltpu
from jax.sharding import PartitionSpec as P

MESH = pl.DeviceIdType.MESH
F32, BF16 = jnp.float32, jnp.bfloat16

TOK = 384
FF = 4096
D = 1024
W = 256
K = FF // W
DELTA = 1
LAG_D = 2
LAG_F = 5
RING = 8
WSLOT = 4
SOON = 3 * FF // 512
AHEAD = 6
OWN_W = 512
OWN = FF // OWN_W


def nt(left, right):
    return lax.dot_general(left, right, (((1,), (1,)), ((), ())), preferred_element_type=F32)


def kernel(
    tok_t, dy_t, hid_hbm, win_hbm, wout_hbm, row_in, col_in, row_out, col_out,
    gt_out, steps_out, new_row_in, new_col_in, new_row_out, new_col_out,
    steps, hid, win, wout_slot, wout_t, gath, dy, lhs, hgo, hgb, gtacc,
    f_send, f_recv, n_send, d_send, nd_recv, keep_d, keep_0,
    gs1, gr1, gs2, gk2, gr2, gs3, gk3, gr3,
    rb, rowm, colm, colz, colm2, colr, rm1, rr1, rm2, rr2,
    load_sem, wout_sem, step_sem, z_ss, z_rs, s_ss, s_rs, y_ss, y_rs, c_ss, c_rs,
    x_ss, f_rs, nd_rs, g_ss, g_rs, e_ss, e_rs, r_ss, r_rs,
):
    dp = lax.axis_index("dp")
    mp = lax.axis_index("mp")
    zlo, x = dp // 4, dp % 4
    zhi, y, c = mp // 8, (mp // 2) % 4, mp % 2

    def dev(zlo_, x_, zhi_, y_, c_):
        return (zlo_ * 4 + x_, zhi_ * 8 + y_ * 2 + c_)

    x_peer = [dev(zlo, (x + i) % 4, zhi, y, c) for i in range(4)]
    y_peer = [dev(zlo, x, zhi, (y + i) % 4, c) for i in range(4)]
    zlo_peer = dev(1 - zlo, x, zhi, y, c)
    zhi_peer = dev(zlo, x, 1 - zhi, y, c)
    diag_peer = dev(1 - zlo, x, 1 - zhi, y, c)
    core_peer = dev(zlo, x, zhi, y, 1 - c)
    pair_peer = dev(zlo, x, 1 - zhi, y, 1 - c)

    def remote(src, dst, ss, rs, peer):
        return pltpu.make_async_remote_copy(
            src_ref=src, dst_ref=dst, send_sem=ss, recv_sem=rs, device_id=peer, device_id_type=MESH
        )

    loads = [
        pltpu.make_async_copy(hid_hbm, hid.at[pl.ds(zlo * TOK, TOK)], load_sem.at[0]),
        pltpu.make_async_copy(win_hbm, win, load_sem.at[1]),
    ]

    def wout_load(k):
        rows = pl.ds(pl.multiple_of(k * W, W), W)
        return pltpu.make_async_copy(wout_hbm.at[rows], wout_slot.at[k % WSLOT], wout_sem.at[k % WSLOT])

    for k in range(WSLOT):
        wout_load(k).start()
    for load in loads:
        load.start()

    barrier = pltpu.get_barrier_semaphore()
    peers = x_peer[1:] + y_peer[1:] + [core_peer, zlo_peer, zhi_peer, pair_peer, diag_peer]
    for peer in peers:
        pl.semaphore_signal(barrier, inc=1, device_id=peer, device_id_type=MESH)
    pl.semaphore_wait(barrier, len(peers))

    toks, dys = pl.ds(0, 64), pl.ds(64, 64)

    def s_copy(i):
        own, rows = (dy_t, dys) if i < 3 else (tok_t, toks)
        peer = (zlo_peer, diag_peer, zhi_peer)[i % 3]
        return remote(own, gath.at[zhi, y, c, zlo, rows], s_ss.at[i], s_rs.at[i], peer)

    far = (zhi + zlo) % 2

    def place(piece):
        if isinstance(piece, int) and piece >= 4:
            return zlo, piece - 4, toks
        second = piece // 2
        lo = (zlo + piece + second) % 2
        return (zhi + second) % 2, lo, dys

    def y_copy(piece, i):
        h, lo, rows = place(piece)
        part = gath.at[h, y, c, lo, rows]
        return remote(part, part, y_ss.at[piece], y_rs.at[piece], y_peer[i])

    def y_all(piece):
        h, lo, rows = place(piece)
        part = gath.at[h, pl.ds(0, 3), c, lo, rows]
        return remote(part, part, y_ss.at[piece], y_rs.at[piece], y_peer[1])

    def c_copy(piece):
        h, lo, rows = place(piece)
        part = gath.at[h, :, c, lo, rows]
        return remote(part, part, c_ss.at[piece], c_rs.at[piece], core_peer)

    def y_start(piece):
        for i in (2, 1, 3):
            y_copy(piece, i).start()

    def z_copy(k):
        cols = pl.ds(pl.multiple_of(k * W, W), W)
        return remote(
            hid_hbm.at[:, cols], hid.at[pl.ds(zlo * TOK, TOK), cols], z_ss.at[0], z_rs.at[k], zlo_peer
        )

    for i in (0, 1, 2):
        s_copy(i).start()
    gath[zhi, y, c, zlo, dys] = dy_t[...]
    y_start(0)

    @pl.when(far == 0)
    def _():
        s_copy(5).start()

    @pl.when(far == 1)
    def _():
        s_copy(3).start()
        s_copy(4).start()

    for k in range(AHEAD):
        z_copy(k).start()

    gath[zhi, y, c, zlo, toks] = tok_t[...]

    @pl.when(far == 0)
    def _():
        s_copy(0).wait_recv()
        y_start(1)
        s_copy(1).wait_recv()
        y_start(2)
        s_copy(2).wait_recv()
        y_start(3)

    @pl.when(far == 1)
    def _():
        s_copy(1).wait_recv()
        y_start(2)
        s_copy(2).wait_recv()
        y_start(3)
        s_copy(0).wait_recv()
        y_start(1)

    @pl.when(far == 0)
    def _():
        s_copy(3).wait_recv()

    @pl.when(far == 1)
    def _():
        s_copy(4).wait_recv()
        s_copy(5).wait_recv()

    y_start(4)
    y_start(5)

    def row_block(row):
        return jnp.broadcast_to(row[...], (128, 128)).T

    rb[0] = row_block(row_in)
    rb[1] = row_block(col_out)
    rowm[...] = jnp.zeros_like(rowm)

    def pass_to_core(piece):
        y_all(piece).wait_recv()
        c_copy(piece).start()

    def assemble(mat):
        for r in range(4):
            owner = (x + r) % 4
            for core in range(2):
                for lo in range(2):
                    lhs[mat, pl.ds(r * 128 + core * 64, 64), pl.ds(lo * TOK, TOK)] = gath[
                        zlo, owner, core, lo, pl.ds(64 * mat, 64), :
                    ]

    def transpose_dy():
        for h in range(2):
            for yy in range(4):
                for lo in range(2):
                    both = jnp.concatenate(
                        [gath[h, yy, 0, lo, 64:128, :], gath[h, yy, 1, lo, 64:128, :]], axis=0
                    )
                    dy[pl.ds(lo * TOK, TOK), pl.ds((h * 4 + yy) * 128, 128)] = both.astype(F32).T.astype(BF16)

    def transpose_wout(k, carry):
        wout_load(k).wait()
        cols = pl.ds(pl.multiple_of(k * W, W), W)
        wout_t[:, cols] = wout_slot[k % WSLOT].T

        @pl.when(k + WSLOT < K)
        def _():
            wout_load(k + WSLOT).start()

        return carry

    lax.fori_loop(0, K // 2, transpose_wout, 0)
    first, rest = 2 * far, 2 * (1 - far)
    pass_to_core(first)
    pass_to_core(first + 1)
    c_copy(first).wait_recv()
    c_copy(first + 1).wait_recv()
    assemble(1)
    loads[0].wait()

    toward = [(x_peer[1], x_peer[3]), (x_peer[3], x_peer[1])]

    def f_copy(mat, k):
        return remote(f_send.at[mat, k], f_recv.at[mat, k], x_ss.at[0], f_rs.at[mat, k], toward[mat][0])

    def n_copy(mat, k):
        return remote(n_send.at[mat, k], nd_recv.at[mat, k, 0], x_ss.at[1], nd_rs.at[mat, k], toward[mat][1])

    def d_copy(mat, k):
        return remote(d_send.at[mat, k], nd_recv.at[mat, k, 1], x_ss.at[2], nd_rs.at[mat, k], toward[mat][0])

    def products(mat, k, right):
        part = jnp.dot(lhs[mat], right, preferred_element_type=F32)
        near, back = (3, 1) if mat == 0 else (1, 3)
        slot = k % RING
        f_send[mat, k] = part[256:384].astype(BF16)
        f_copy(mat, k).start()
        n_send[mat, k] = part[near * 128 : near * 128 + 128].astype(BF16)
        n_copy(mat, k).start()
        keep_d[mat, slot] = part[back * 128 : back * 128 + 128]
        keep_0[mat, slot] = part[0:128]

    def pass_on(mat, k):
        f_copy(mat, k).wait_recv()
        d_send[mat, k] = (keep_d[mat, k % RING] + f_recv[mat, k].astype(F32)).astype(BF16)
        d_copy(mat, k).start()

    def step_copy(mat, k):
        cols = pl.ds(pl.multiple_of(k * W, W), W)
        return pltpu.make_async_copy(steps.at[mat, :, cols], steps_out.at[mat, :, cols], step_sem.at[0])

    def finish(mat, k):
        both = nd_recv.at[mat, k]
        remote(both, both, x_ss.at[1], nd_rs.at[mat, k], toward[mat][1]).wait_recv()
        lanes = col_in if mat == 0 else row_out
        for h in range(W // 128):
            cut = pl.ds(h * 128, 128)
            g = (
                keep_0[mat, k % RING, :, cut]
                + nd_recv[mat, k, 0, :, cut].astype(F32)
                + nd_recv[mat, k, 1, :, cut].astype(F32)
            )
            block = k * (W // 128) + h
            nu = jnp.minimum(rb[mat], lanes[pl.ds(block, 1), :]) + g * g
            step = g * lax.rsqrt(nu)
            steps[mat, :, pl.ds(pl.multiple_of(block * 128, 128), 128)] = step.astype(BF16)
            rowm[mat] = jnp.maximum(rowm[mat], nu)
            last = block // SOON
            row = (1 - mat) * (SOON - last * (2 * SOON - FF // 128)) + last * SOON + block
            colm[pl.ds(row, 1), :] = jnp.max(nu, axis=0, keepdims=True)
        step_copy(mat, k).start()

    def hidden_grad(lo, start, width):
        cols = pl.ds(pl.multiple_of(start, width), width)
        rows = pl.ds(pl.multiple_of(lo * TOK, TOK), TOK)
        back = jnp.dot(dy[rows, :], wout_t[:, cols], preferred_element_type=F32)
        return jnp.where(hid[rows, cols] > 0, back, F32(0.0)).astype(BF16)

    def own_grad(j):
        cols = pl.ds(pl.multiple_of(j * OWN_W, OWN_W), OWN_W)
        hgo[:, cols] = hidden_grad(zlo, j * OWN_W, OWN_W)

    def own_term(j):
        cols = pl.ds(pl.multiple_of(j * OWN_W, OWN_W), OWN_W)
        gtacc[...] += nt(win[:, cols], hgo[:, cols])

    def g_copy(i):
        if i == 0:
            return remote(gs1, gr1, g_ss.at[0], g_rs.at[0], core_peer)
        if i < 4:
            return remote(gs2.at[(y + i) % 4], gr2.at[i - 1], g_ss.at[1], g_rs.at[1], y_peer[i])
        return remote(gs3, gr3, g_ss.at[2], g_rs.at[2], zhi_peer)

    def g_all():
        return remote(gs2.at[pl.ds(0, 3)], gr2, g_ss.at[1], g_rs.at[1], y_peer[1])

    def gt_rows(j, core):
        return gtacc[pl.ds(pl.multiple_of(j * 128 + core * 64, 64), 64), :]

    def gt_stage(i):
        if i == 0:
            for j in range(8):
                gs1[j] = gt_rows(j, 1 - c).astype(BF16)
            g_copy(0).start()
        elif i == 1:
            g_copy(0).wait_recv()
            for h in range(2):
                for yy in range(4):
                    gs2[yy, h] = (gt_rows(h * 4 + yy, c) + gr1[h * 4 + yy].astype(F32)).astype(BF16)
                gk2[h] = gt_rows(h * 4 + y, c) + gr1[h * 4 + y].astype(F32)
            for j in (1, 2, 3):
                g_copy(j).start()
        elif i == 2:
            g_all().wait_recv()

            def total(h):
                return gk2[h] + gr2[0, h].astype(F32) + gr2[1, h].astype(F32) + gr2[2, h].astype(F32)

            gs3[...] = total(1 - zhi).astype(BF16)
            gk3[...] = total(zhi)
            g_copy(4).start()
        else:
            g_copy(4).wait_recv()
            gt_out[...] = (gk3[...] + gr3[...].astype(F32)).astype(BF16)
            g_copy(0).wait_send()
            g_all().wait_send()
            g_copy(4).wait_send()

    def between(value, low, high):
        return jnp.logical_and(value >= low, value < high)

    early, late = pl.ds(0, 2 * SOON), pl.ds(2 * SOON, 2 * FF // 128 - 2 * SOON)

    def col_pair(part, j):
        return remote(colm.at[part], colz.at[part], e_ss.at[j], e_rs.at[j], zlo_peer)

    def col_ring(part, j, i):
        return remote(colm2.at[part], colr.at[i - 1, part], e_ss.at[2 + j], e_rs.at[2 + j], x_peer[i])

    def col_all(part, j):
        return remote(colr.at[:, part], colr.at[:, part], e_ss.at[2 + j], e_rs.at[2 + j], x_peer[1])

    def pass_columns(part, j):
        col_pair(part, j).wait()
        colm2[part] = jnp.maximum(colm[part], colz[part])
        for i in (2, 1, 3):
            col_ring(part, j, i).start()

    def turn(i, carry):
        for mat, first in ((1, 0), (0, DELTA)):

            @pl.when(between(i - first - LAG_D, 0, K))
            def _():
                pass_on(mat, i - first - LAG_D)

            @pl.when(between(i - first - LAG_F, 0, K))
            def _():
                finish(mat, i - first - LAG_F)

        @pl.when(i < K)
        def _():
            z_copy(i).wait_recv()

            @pl.when(i + AHEAD < K)
            def _():
                z_copy(i + AHEAD).start()

            cols = pl.ds(pl.multiple_of(i * W, W), W)
            pre = hid[:, cols]
            products(1, i, jnp.maximum(pre, jnp.zeros_like(pre)))

        p = i - DELTA

        @pl.when(p == 0)
        def _():
            pass_to_core(rest)
            pass_to_core(rest + 1)
            c_copy(rest).wait_recv()
            c_copy(rest + 1).wait_recv()
            transpose_dy()
            pass_to_core(4)
            pass_to_core(5)

        @pl.when(between(p, 0, OWN))
        def _():
            own_grad(p)

        @pl.when(between(p, 0, K))
        def _():
            cols = pl.ds(pl.multiple_of(p * W, W), W)
            hgb[pl.ds(pl.multiple_of(zlo * TOK, TOK), TOK), :] = hgo[:, cols]
            hgb[pl.ds(pl.multiple_of((1 - zlo) * TOK, TOK), TOK), :] = hidden_grad(1 - zlo, p * W, W)

        @pl.when(p == 0)
        def _():
            c_copy(4).wait_recv()
            c_copy(5).wait_recv()
            assemble(0)

        @pl.when(between(p, 0, K))
        def _():
            products(0, p, hgb[...])

        @pl.when(p == 0)
        def _():
            loads[1].wait()
            gtacc[...] = jnp.zeros_like(gtacc)
            lax.fori_loop(K // 2, K, transpose_wout, 0)

        @pl.when(between(p, 0, OWN))
        def _():
            own_term(p)

        for s, at in enumerate((OWN, OWN + 1, OWN + 3, OWN + 5)):

            @pl.when(p == at)
            def _():
                gt_stage(s)

        @pl.when(i == K * 3 // 4 - 1 + DELTA + LAG_F)
        def _():
            col_pair(early, 0).start()

        @pl.when(i == K * 3 // 4 + 1 + DELTA + LAG_F)
        def _():
            pass_columns(early, 0)

        return carry

    lax.fori_loop(0, K + DELTA + LAG_F, turn, 0)

    col_pair(late, 1).start()
    rm1[...] = jnp.zeros_like(rm1)
    for mat in range(2):
        rm1[mat : mat + 1, :] = jnp.max(rowm[mat].T, axis=0, keepdims=True)

    def row_copy(i):
        if i < 3:
            return remote(rm1, rr1.at[i], r_ss.at[0], r_rs.at[0], (core_peer, zhi_peer, pair_peer)[i])
        return remote(rm2, rr2.at[i - 3], r_ss.at[1], r_rs.at[1], y_peer[i - 2])

    for i in (2, 1, 0):
        row_copy(i).start()
    row_1 = remote(rr1, rr1, r_ss.at[0], r_rs.at[0], core_peer)
    row_2 = remote(rr2, rr2, r_ss.at[1], r_rs.at[1], y_peer[1])
    pass_columns(late, 1)
    row_1.wait_recv()
    rm2[...] = jnp.maximum(jnp.maximum(rm1[...], rr1[0]), jnp.maximum(rr1[1], rr1[2]))
    for i in (4, 3, 5):
        row_copy(i).start()

    for i in range(3):
        s_copy(i).wait_send()

    @pl.when(far == 0)
    def _():
        s_copy(5).wait_send()

    @pl.when(far == 1)
    def _():
        s_copy(3).wait_send()
        s_copy(4).wait_send()

    for piece in range(6):
        y_all(piece).wait_send()
        c_copy(piece).wait_send()

    own_rows = hid.at[pl.ds(zlo * TOK, TOK)]
    remote(hid_hbm, own_rows, z_ss.at[0], z_rs.at[0], zlo_peer).wait_send()
    remote(f_send, f_recv, x_ss.at[0], f_rs.at[0, 0], x_peer[1]).wait_send()
    remote(n_send, f_recv, x_ss.at[1], f_rs.at[0, 0], x_peer[1]).wait_send()
    remote(d_send, f_recv, x_ss.at[2], f_rs.at[0, 0], x_peer[1]).wait_send()

    pltpu.make_async_copy(steps, steps_out, step_sem.at[0]).wait()

    col_all(early, 0).wait()
    col_all(late, 1).wait()
    top = colm2[...]
    for i in range(3):
        top = jnp.maximum(top, colr[i])
    rest_rows = FF // 128 - SOON
    new_row_out[...] = jnp.concatenate([top[0:SOON], top[2 * SOON : 2 * SOON + rest_rows]], axis=0)
    new_col_in[...] = jnp.concatenate([top[SOON : 2 * SOON], top[2 * SOON + rest_rows :]], axis=0)
    row_1.wait_send()
    row_2.wait()
    top = jnp.maximum(jnp.maximum(rm2[...], rr2[0]), jnp.maximum(rr2[1], rr2[2]))
    new_row_in[...] = top[0:1]
    new_col_out[...] = top[1:2]


def write_out(steps_in, steps_out, gt, nri, nci, nro, nco, o_gt, o_in, o_out, o_nri, o_nci, o_nro, o_nco):
    o_in[...] = steps_in[0].astype(F32)
    o_out[...] = steps_out[0].astype(F32).T

    @pl.when(pl.program_id(0) == 0)
    def _():
        o_gt[...] = gt[...]
        o_nri[...] = nri[...]
        o_nci[...] = nci[...]
        o_nro[...] = nro[...]
        o_nco[...] = nco[...]


def on_device(tokens, grad_out, hidden_pre, w_in, w_out, row_in, col_in, row_out, col_out):
    vmem = pl.BlockSpec(memory_space=pltpu.VMEM)
    hbm = pl.BlockSpec(memory_space=pl.ANY)
    dma = pltpu.SemaphoreType.DMA
    rows = FF // 128
    wire = pltpu.VMEM((2, K, 128, W), BF16)
    kept = pltpu.VMEM((2, RING, 128, W), F32)
    small = (
        jax.ShapeDtypeStruct((64, TOK), BF16),
        jax.ShapeDtypeStruct((1, 128), F32),
        jax.ShapeDtypeStruct((rows, 128), F32),
        jax.ShapeDtypeStruct((rows, 128), F32),
        jax.ShapeDtypeStruct((1, 128), F32),
    )
    gt, steps, nri, nci, nro, nco = pl.pallas_call(
        kernel,
        out_shape=small[:1] + (jax.ShapeDtypeStruct((2, 128, FF), BF16),) + small[1:],
        in_specs=[vmem, vmem, hbm, hbm, hbm, vmem, vmem, vmem, vmem],
        out_specs=(vmem, hbm, vmem, vmem, vmem, vmem),
        scratch_shapes=[
            pltpu.VMEM((2, 128, FF), BF16),
            pltpu.VMEM((2 * TOK, FF), BF16),
            pltpu.VMEM((D, FF), BF16),
            pltpu.VMEM((WSLOT, W, D), BF16),
            pltpu.VMEM((D, FF), BF16),
            pltpu.VMEM((2, 4, 2, 2, 128, TOK), BF16),
            pltpu.VMEM((2 * TOK, D), BF16),
            pltpu.VMEM((2, 512, 2 * TOK), BF16),
            pltpu.VMEM((TOK, FF), BF16),
            pltpu.VMEM((2 * TOK, W), BF16),
            pltpu.VMEM((D, TOK), F32),
            wire, wire, wire, wire,
            pltpu.VMEM((2, K, 2, 128, W), BF16),
            kept, kept,
            pltpu.VMEM((8, 64, TOK), BF16),
            pltpu.VMEM((8, 64, TOK), BF16),
            pltpu.VMEM((4, 2, 64, TOK), BF16),
            pltpu.VMEM((2, 64, TOK), F32),
            pltpu.VMEM((3, 2, 64, TOK), BF16),
            pltpu.VMEM((64, TOK), BF16),
            pltpu.VMEM((64, TOK), F32),
            pltpu.VMEM((64, TOK), BF16),
            pltpu.VMEM((2, 128, 128), F32),
            pltpu.VMEM((2, 128, 128), F32),
            pltpu.VMEM((2 * rows, 128), F32),
            pltpu.VMEM((2 * rows, 128), F32),
            pltpu.VMEM((2 * rows, 128), F32),
            pltpu.VMEM((3, 2 * rows, 128), F32),
            pltpu.VMEM((8, 128), F32),
            pltpu.VMEM((3, 8, 128), F32),
            pltpu.VMEM((8, 128), F32),
            pltpu.VMEM((3, 8, 128), F32),
            dma((2,)), dma((WSLOT,)), dma((1,)),
            dma((1,)), dma((K,)),
            dma((6,)), dma((6,)),
            dma((6,)), dma((6,)),
            dma((6,)), dma((6,)),
            dma((3,)), dma((2, K)), dma((2, K)),
            dma((3,)), dma((3,)),
            dma((4,)), dma((4,)),
            dma((2,)), dma((2,)),
        ],
        compiler_params=pltpu.CompilerParams(
            collective_id=0, has_side_effects=True, vmem_limit_bytes=63 * 2**20
        ),
        name="ffn_backward",
    )(
        tokens.T, grad_out.T, hidden_pre, w_in, w_out,
        row_in.reshape(1, 128), col_in.reshape(rows, 128), row_out.reshape(rows, 128), col_out.reshape(1, 128),
    )

    parts = 2
    wide = FF // parts

    def whole(shape):
        return pl.BlockSpec(shape.shape, lambda j: (0,) * len(shape.shape))

    gt, step_in, step_out, nri, nci, nro, nco = pl.pallas_call(
        write_out,
        grid=(parts,),
        out_shape=small[:1]
        + (jax.ShapeDtypeStruct((128, FF), F32), jax.ShapeDtypeStruct((FF, 128), F32))
        + small[1:],
        in_specs=[
            pl.BlockSpec((1, 128, wide), lambda j: (0, 0, j)),
            pl.BlockSpec((1, 128, wide), lambda j: (1, 0, j)),
        ]
        + [whole(shape) for shape in small],
        out_specs=(
            whole(small[0]),
            pl.BlockSpec((128, wide), lambda j: (0, j)),
            pl.BlockSpec((wide, 128), lambda j: (j, 0)),
        )
        + tuple(whole(shape) for shape in small[1:]),
        name="write_out",
    )(steps, steps, gt, nri, nci, nro, nco)
    return (
        gt.T, step_in, step_out,
        nri.reshape(128), nci.reshape(FF), nro.reshape(FF), nco.reshape(128),
    )


def solution(mesh):
    in_specs = (
        P("dp", "mp"),
        P("dp", "mp"),
        P("dp", "mp"),
        P(None, "mp"),
        P("mp", None),
        P("dp"),
        P("mp"),
        P("mp"),
        P("dp"),
    )
    out_specs = (P("dp", "mp"), P("dp", "mp"), P("mp", "dp"), P("dp"), P("mp"), P("mp"), P("dp"))
    return jax.shard_map(
        on_device, mesh=mesh, in_specs=in_specs, out_specs=out_specs, check_vma=False
    )
```
